32 devices in a mesh: groups: 2 (over y), ctx: 4 (over z), tp: 4 (over x, core).
Axes of the slice: x: 2, y: 2, z: 4, core: 2. Of those that a mesh axis runs over, the one named last changes fastest.
Arguments:
- q_in: bfloat16 [1024, 8192], P(('groups', 'ctx'), 'tp'), parts along dimension 0, may hold values from -6 to 6
- k_in: bfloat16 [1024, 8192], P(('groups', 'ctx'), 'tp'), parts along dimension 0, may hold values from -6 to 6
- v_in: bfloat16 [1024, 8192], P(('groups', 'ctx'), 'tp'), parts along dimension 0, may hold values from -6 to 6
- short_filters: float32 [3, 512, 7], P(None, 'tp'), may hold values from -2.5 to 2.5
- rates: float32 [16, 8192], P(None, 'tp'), may hold values from 1.953125e-05 to 0.0625
- residues: float32 [16, 8192], P(None, 'tp'), may hold values from -2.5 to 2.5
- out_weight: bfloat16 [8192, 4096], P('tp', 'ctx'), may hold values from -0.0625 to 0.0625
- cotangent: bfloat16 [1024, 4096], P(('groups', 'ctx'), 'tp'), parts along dimension 0, may hold values from -6 to 6
Outputs:
- out: bfloat16 [1024, 4096], P(('groups', 'ctx'), 'tp'), parts along dimension 0
- grad_q: bfloat16 [1024, 8192], P(('groups', 'ctx'), 'tp'), parts along dimension 0
- grad_k: bfloat16 [1024, 8192], P(('groups', 'ctx'), 'tp'), parts along dimension 0
- grad_v: bfloat16 [1024, 8192], P(('groups', 'ctx'), 'tp'), parts along dimension 0
- grad_short: float32 [6, 512, 7], P('groups', 'tp'), parts along dimension 0
The draws below stay inside these ranges and needn't reach their ends.
There are 2 independent parts, one for each index of `groups`. The reference program is written for one: setup_inputs(seed, part) draws one part's arguments, and reference() takes and returns one part's arrays. A program takes and returns all parts, laid end to end along the dimension named above; an argument that names none is the same for every part. Nothing has to cross between parts.
All inputs are finite; a program needn't handle non-finite values.
Results may differ from the reference program's by a relative error of at most 0.013.
Values may be sent and summed in bfloat16 or wider, within the bound.
A program may use at most 192 MiB of HBM per device.

```python
import math
import jax
import jax.numpy as jnp
from jax import lax

D = 8192
ORDER = 16
SHORT = 7
CH_GROUP = 16
OUTW = 4096
TOKENS = 512
GROUPS = 512
N_TP = 4


def draw_rates(key, part):
    low_end = math.log(0.01 / TOKENS)
    high_end = math.log(1.0 / 16.0)
    return jnp.exp(jax.random.uniform(key, (ORDER, D), jnp.float32, low_end, high_end))


def levels(rng, extent, pieces, smallest, high):
    def one(position, blocks):
        draws = jax.random.uniform(jax.random.fold_in(jax.random.fold_in(rng, 6), position), (blocks,), jnp.float32, smallest / len(pieces), high / len(pieces))
        return jnp.repeat(jnp.exp(draws), extent[position] // blocks).reshape((-1,) + (1,) * (len(extent) - position - 1))

    level = one(*pieces[0])
    for cut in pieces[1:]:
        level = level * one(*cut)
    return level


def scatter_about(rng, dims, spread, reach, shards=(), dtype=jnp.bfloat16):
    drawn = jax.random.normal(rng, dims, jnp.float32) * spread
    if len(shards) > 0:
        drawn = levels(rng, dims, shards, -0.22, 0.18) * drawn
    return jnp.clip(drawn, min=-reach, max=reach).astype(dtype)


def setup_inputs(seed: int = 0, part: int = 0) -> dict:
    seeds = jax.random.split(jax.random.key(seed), 9)
    part_keys = jax.random.split(jax.random.fold_in(seeds[8], part), 9)
    return {
        "q_in": scatter_about(part_keys[0], (TOKENS, D), 1.0, 6.0, ((0, 4), (1, 4))),
        "k_in": scatter_about(part_keys[1], (TOKENS, D), 1.0, 6.0, ((0, 4), (1, 4))),
        "v_in": scatter_about(part_keys[2], (TOKENS, D), 1.0, 6.0, ((0, 4), (1, 4))),
        "short_filters": scatter_about(seeds[3], (3, GROUPS, SHORT), 0.4, 2.5, ((1, 4),), jnp.float32),
        "rates": draw_rates(jax.random.fold_in(seeds[8], 71), part),
        "residues": scatter_about(seeds[5], (ORDER, D), 0.25, 2.5, ((1, 4),), jnp.float32),
        "out_weight": scatter_about(seeds[6], (D, OUTW), D ** -0.5, 0.0625, ((0, 4), (1, 4))),
        "cotangent": scatter_about(part_keys[7], (TOKENS, OUTW), 1.0, 6.0, ((0, 4), (1, 4))),
    }


def short_filter(inputs, filters):
    length = inputs.shape[0]
    filter_taps = filters.shape[1]
    filter_rows = jnp.repeat(filters, CH_GROUP, axis=0)
    padded = jnp.pad(inputs, ((filter_taps - 1, 0), (0, 0)))
    result = jnp.zeros(inputs.shape, jnp.float32)
    for shift_by in range(filter_taps):
        start = filter_taps - 1 - shift_by
        result = result + filter_rows[:, shift_by] * padded[start:start + length]
    return (result, padded)

def filter_adjoint(grads, padded, filters):
    length = grads.shape[0]
    filter_taps = filters.shape[1]
    filter_rows = jnp.repeat(filters, CH_GROUP, axis=0)
    grad_padded = jnp.pad(grads, ((0, filter_taps - 1), (0, 0)))
    input_grad = jnp.zeros(grads.shape, jnp.float32)
    filter_terms = []
    for shift_by in range(filter_taps):
        input_grad = input_grad + filter_rows[:, shift_by] * grad_padded[shift_by:shift_by + length]
        start = filter_taps - 1 - shift_by
        summed = lax.optimization_barrier(jnp.sum(grads * padded[start:start + length], axis=0))
        filter_terms.append(lax.optimization_barrier(jnp.sum(summed.reshape(-1, CH_GROUP), axis=1)))
    return (input_grad, jnp.stack(filter_terms, axis=1) / length)

def reference(q_in, k_in, v_in, short_filters, rates, residues, out_weight, cotangent):
    query_conv, query_padded = short_filter(q_in.astype(jnp.float32), short_filters[0])
    key_conv, key_padded = short_filter(k_in.astype(jnp.float32), short_filters[1])
    value_conv, value_padded = short_filter(v_in.astype(jnp.float32), short_filters[2])
    gated = key_conv * value_conv
    decay = jnp.exp(-rates)
    scaled = residues * jnp.sqrt(-jnp.expm1(-2.0 * rates))
    zero_state = jnp.zeros((ORDER, D), jnp.float32)

    def advance(state, column):
        state = decay * state + column[None, :]
        return (state, lax.optimization_barrier(jnp.sum(scaled * state, axis=0)))
    _, mixed = lax.scan(advance, zero_state, gated)
    product = (query_conv * mixed).astype(jnp.bfloat16)
    block_width = D // N_TP
    total = jnp.zeros((product.shape[0], OUTW), jnp.float32)
    for block_index in range(N_TP):
        lower = block_index * block_width
        partial_value = jnp.dot(product[:, lower:lower + block_width], out_weight[lower:lower + block_width], preferred_element_type=jnp.float32)
        rounded = lax.optimization_barrier(partial_value.astype(jnp.bfloat16))
        total = total + rounded.astype(jnp.float32)
    out = total.astype(jnp.bfloat16)
    grad_product = jnp.dot(cotangent, out_weight.T, preferred_element_type=jnp.float32)
    grad_query = grad_product * mixed
    grad_mixed = grad_product * query_conv
    _, grad_gated = lax.scan(advance, zero_state, grad_mixed, reverse=True)
    grad_key = grad_gated * value_conv
    grad_value = grad_gated * key_conv
    grad_q, filter_q = filter_adjoint(grad_query, query_padded, short_filters[0])
    grad_k, filter_k = filter_adjoint(grad_key, key_padded, short_filters[1])
    grad_v, filter_v = filter_adjoint(grad_value, value_padded, short_filters[2])
    grad_short = jnp.stack([filter_q, filter_k, filter_v], axis=0)
    return (out, grad_q.astype(jnp.bfloat16), grad_k.astype(jnp.bfloat16), grad_v.astype(jnp.bfloat16), grad_short)
```

```python
import functools

import jax
import jax.numpy as jnp
from jax import lax
from jax.experimental import pallas as pl
from jax.experimental.pallas import tpu as pltpu
from jax.sharding import PartitionSpec as P

block_rows = 16


def shifted(shard, axis, by):
    length = lax.axis_size(axis)
    pairs = [(i, i + by) for i in range(length) if 0 <= i + by < length]
    return lax.ppermute(shard, axis, pairs)


def entering(shard, axis, combine, identity, reverse):
    length, index = (lax.axis_size(axis), lax.axis_index(axis))
    everything = jax.tree.map(
        lambda part, kind: lax.all_gather(part.astype(kind), axis),
        shard,
        (jnp.bfloat16, jnp.bfloat16),
    )
    start = jax.tree.map(
        lambda part, zero: jnp.broadcast_to(jnp.asarray(zero, part.dtype), part.shape),
        shard,
        identity,
    )

    def lap(k, before):
        at = length - 1 - k if reverse else k
        reached = at > index if reverse else at < index
        new = combine(
            before, jax.tree.map(lambda part, own: part[at].astype(own.dtype), everything, shard)
        )
        return jax.tree.map(lambda a, b: jnp.where(reached, a, b), new, before)

    return lax.fori_loop(0, length, lap, start)


def shortened(shard):
    return jax.tree.map(lambda a: a.astype(jnp.bfloat16) if a.dtype == jnp.float32 else a, shard)


def chain_link(earlier, following):
    return (earlier[0] * following[0], following[0] * earlier[1] + following[1])


def shards(q_in, k_in, v_in, short_filters, rates, residues, out_weight, cotangent):
    length, channels = q_in.shape
    filter_taps = short_filters.shape[2]
    group_count = short_filters.shape[1]
    group_size = channels // group_count
    blocks = length // block_rows
    sequence = length * lax.axis_size("ctx")
    highest = lax.Precision.HIGHEST
    stacked = jnp.stack([q_in, k_in, v_in])
    front_rows = shifted(stacked[:, length - filter_taps + 1 :, :], "ctx", 1)
    extended = jnp.concatenate([front_rows, stacked], axis=1).astype(jnp.float32)
    filter_rows = jnp.repeat(short_filters, group_size, axis=1)
    convolved = jnp.zeros((3, length, channels), jnp.float32)
    for shift_by in range(filter_taps):
        start = filter_taps - 1 - shift_by
        convolved = (
            convolved + filter_rows[:, None, :, shift_by] * extended[:, start : start + length, :]
        )
    query_conv = convolved[0]
    key_conv = convolved[1]
    value_conv = convolved[2]
    gated = key_conv * value_conv
    offsets = jnp.arange(block_rows, dtype=jnp.float32)
    scaled = residues * jnp.sqrt(-jnp.expm1(-2.0 * rates))
    powers = jnp.exp(-rates[None] * offsets[:, None, None])
    kernel = jnp.sum(powers * scaled[None], axis=1)
    lag_table = (
        jnp.arange(block_rows, dtype=jnp.int32)[:, None]
        - jnp.arange(block_rows, dtype=jnp.int32)[None, :]
    )
    toeplitz = jnp.where((lag_table >= 0)[:, :, None], kernel[jnp.maximum(lag_table, 0)], 0.0)
    end_powers = jnp.exp(-rates[None] * (block_rows - 1.0 - offsets)[:, None, None])
    lead_powers = scaled[None] * jnp.exp(-rates[None] * (offsets + 1.0)[:, None, None])
    tail_powers = scaled[None] * jnp.exp(-rates[None] * (block_rows - offsets)[:, None, None])
    block_index = jnp.arange(blocks, dtype=jnp.float32)
    block_decay = jnp.broadcast_to(jnp.exp(-rates * block_rows)[None], (blocks,) + rates.shape)
    entry_decay = jnp.exp(-rates[None] * (block_rows * block_index)[:, None, None])
    exit_decay = jnp.exp(-rates[None] * (block_rows * (blocks - 1.0 - block_index))[:, None, None])
    piece_decay = jnp.exp(-rates * length)
    identity = (jnp.ones_like(rates), jnp.zeros_like(rates))
    gated_blocks = gated.reshape(blocks, block_rows, channels)
    block_states = jnp.einsum("snc,bsc->bnc", end_powers, gated_blocks, precision=highest)
    prefix = lax.associative_scan(chain_link, (block_decay, block_states), axis=0)[1]
    local_end = prefix[-1]
    state_in = entering((piece_decay, local_end), "ctx", chain_link, identity, False)[1]
    earlier_states = jnp.concatenate([jnp.zeros_like(prefix[:1]), prefix[:-1]], axis=0)
    entry_states = earlier_states + entry_decay * state_in[None]
    mixed = jnp.einsum("tsc,bsc->btc", toeplitz, gated_blocks, precision=highest)
    mixed = mixed + jnp.einsum("tnc,bnc->btc", lead_powers, entry_states, precision=highest)
    mixed = mixed.reshape(length, channels)
    product = (query_conv * mixed).astype(jnp.bfloat16)
    weights = lax.all_gather(out_weight, "ctx", axis=1, tiled=True)
    partial_value = jnp.dot(product, weights, preferred_element_type=jnp.float32)
    output = lax.psum_scatter(
        partial_value.astype(jnp.bfloat16), "tp", scatter_dimension=1, tiled=True
    )
    seed = lax.all_gather(cotangent, "tp", axis=1, tiled=True)
    grad_product = lax.dot_general(
        seed, weights, (((1,), (1,)), ((), ())), preferred_element_type=jnp.float32
    )
    grad_query = grad_product * mixed
    grad_mixed = (grad_product * query_conv).reshape(blocks, block_rows, channels)
    block_adjoint = jnp.einsum("snc,bsc->bnc", powers, grad_mixed, precision=highest)
    suffix = lax.associative_scan(chain_link, (block_decay, block_adjoint), reverse=True, axis=0)[1]
    local_begin = suffix[0]
    adjoint_in = entering((piece_decay, local_begin), "ctx", chain_link, identity, True)[1]
    later_adjoint = jnp.concatenate([suffix[1:], jnp.zeros_like(suffix[:1])], axis=0)
    exit_adjoint = later_adjoint + exit_decay * adjoint_in[None]
    grad_gated = jnp.einsum("tsc,btc->bsc", toeplitz, grad_mixed, precision=highest)
    grad_gated = grad_gated + jnp.einsum(
        "snc,bnc->bsc", tail_powers, exit_adjoint, precision=highest
    )
    grad_gated = grad_gated.reshape(length, channels)
    grads = jnp.stack([grad_query, grad_gated * value_conv, grad_gated * key_conv])
    back_rows = shifted(shortened(grads[:, : filter_taps - 1, :]), "ctx", -1)
    grad_extended = jnp.concatenate([grads, back_rows], axis=1)
    input_grads = jnp.zeros((3, length, channels), jnp.float32)
    filter_terms = []
    for shift_by in range(filter_taps):
        input_grads = (
            input_grads
            + filter_rows[:, None, :, shift_by] * grad_extended[:, shift_by : shift_by + length, :]
        )
        start = filter_taps - 1 - shift_by
        filter_terms.append(jnp.sum(grads * extended[:, start : start + length, :], axis=1))
    local_filter = jnp.stack(filter_terms, axis=1)
    local_filter = (
        jnp.sum(local_filter.reshape(3, filter_taps, group_count, group_size), axis=3) / sequence
    )
    local_filter = jnp.transpose(local_filter, (0, 2, 1))
    grad_short = lax.psum(local_filter, "ctx")
    input_grads = input_grads.astype(jnp.bfloat16)
    return (output, input_grads[0], input_grads[1], input_grads[2], grad_short)


LANES = 128
MESH = pl.DeviceIdType.MESH


def remote(src, dst, send, recv, where):
    return pltpu.make_async_remote_copy(
        src_ref=src, dst_ref=dst, send_sem=send, recv_sem=recv, device_id=where, device_id_type=MESH
    )


def fused_kernel(
    n,
    q_ref,
    k_ref,
    v_ref,
    taps_ref,
    rates_ref,
    scaled_ref,
    w_ref,
    cot_ref,
    out_ref,
    gq_ref,
    gk_ref,
    gv_ref,
    gs_ref,
    halo,
    xp,
    conv,
    seq_in,
    seq_out,
    end_mine,
    end_in,
    entry,
    cot_all,
    part,
    part_in,
    prod_all,
    opart,
    opart_in,
    osum,
    ofin,
    ge,
    ghalo_mine,
    ghalo,
    fsum,
    fs_mine,
    fs_in,
    cot_sem,
    cot_send,
    cot_recv,
    halo_send,
    halo_recv,
    state_send,
    state_recv,
    adj_send,
    adj_recv,
    rs_send,
    rs_recv,
    ag_send,
    ag_recv,
    ors_send,
    ors_recv,
    fin_sem,
    gh_send,
    gh_recv,
    fs_send,
    fs_recv,
):
    c = lax.axis_index("ctx")
    p = lax.axis_index("tp")
    L, C = q_ref.shape
    N = w_ref.shape[1]
    taps = taps_ref.shape[1]
    ncb = C // LANES
    modes = rates_ref.shape[0] // ncb
    halves = ncb // 8
    inputs = (q_ref, k_ref, v_ref)

    def ctx_at(d):
        return lax.rem(c + d + n, n)

    def tp_at(d):
        return lax.rem(p + d + n, n)

    def rows_of(i):
        return pl.ds(pl.multiple_of(i * L, L), L)

    def cols_of(i, width=LANES):
        return pl.ds(pl.multiple_of(i * width, width), width)

    barrier = pltpu.get_barrier_semaphore()
    for d in range(1, n):
        pl.semaphore_signal(barrier, inc=1, device_id={"ctx": ctx_at(d)}, device_id_type=MESH)
        pl.semaphore_signal(barrier, inc=1, device_id={"tp": tp_at(d)}, device_id_type=MESH)

    @pl.when(c != p)
    def _():
        pl.semaphore_signal(barrier, inc=1, device_id={"ctx": p, "tp": c}, device_id_type=MESH)

    @pl.when(c != p)
    def _():
        pl.semaphore_wait(barrier, 2 * (n - 1) + 1)

    @pl.when(c == p)
    def _():
        pl.semaphore_wait(barrier, 2 * (n - 1))

    halo_copies = [
        remote(
            x.at[pl.ds(L - 16, 16), :],
            halo.at[b],
            halo_send.at[b],
            halo_recv.at[b],
            {"ctx": ctx_at(1)},
        )
        for b, x in enumerate(inputs)
    ]

    @pl.when(c < n - 1)
    def _():
        for copy in halo_copies:
            copy.start()

    cot_turn = remote(
        cot_ref, cot_all.at[rows_of(c), :], cot_sem.at[0], cot_sem.at[1], {"ctx": p, "tp": c}
    )
    cot_keep = pltpu.make_async_copy(cot_ref, cot_all.at[rows_of(c), :], cot_sem.at[2])

    @pl.when(c != p)
    def _():
        cot_turn.start()

    @pl.when(c == p)
    def _():
        cot_keep.start()

    @pl.when(c == 0)
    def _():
        halo[...] = jnp.zeros(halo.shape, halo.dtype)

    @pl.when(c > 0)
    def _():
        for copy in halo_copies:
            copy.wait_recv()

    def conv_block(i, carry):
        col = cols_of(i)
        done = []
        for b, x in enumerate(inputs):
            at = b * ncb + i
            xp[at, 0:8, :] = halo[b, :, col].astype(jnp.float32)[8:16]
            xp[at, 8 : 8 + L, :] = x[:, col].astype(jnp.float32)
            acc = taps_ref[b, 0:1, col] * xp[at, 8 : 8 + L, :]
            for j in range(1, taps):
                acc = acc + taps_ref[b, j : j + 1, col] * xp[at, 8 - j : 8 - j + L, :]
            conv[at] = acc
            done.append(acc)
        seq_in[pl.ds(i, L, stride=ncb), :] = done[1] * done[2]
        return carry

    half_blocks = ncb // 2
    lax.fori_loop(0, half_blocks, conv_block, 0)

    @pl.when(c != p)
    def _():
        cot_turn.wait_recv()

    @pl.when(c == p)
    def _():
        cot_keep.wait()

    cot_copies = [
        remote(
            cot_all.at[rows_of(p), :],
            cot_all.at[rows_of(p), :],
            cot_send.at[d - 1],
            cot_recv.at[d - 1],
            {"tp": tp_at(d)},
        )
        for d in range(1, n)
    ]
    for copy in cot_copies:
        copy.start()

    lax.fori_loop(half_blocks, ncb, conv_block, 0)

    def mode_rows(k, h):
        return pl.ds(k * ncb + h * 8, 8)

    def last_state(reverse):
        for h in range(halves):
            lam = [jnp.exp(-rates_ref[mode_rows(k, h), :]) for k in range(modes)]

            def step(t, states):
                for u in range(4):
                    at = 4 * t + u
                    if reverse:
                        at = L - 1 - at
                    x = seq_in[pl.ds(pl.multiple_of(at * ncb + h * 8, 8), 8), :]
                    states = tuple(a * s + x for a, s in zip(lam, states))
                return states

            zero = jnp.zeros((8, LANES), jnp.float32)
            states = lax.fori_loop(0, L // 4, step, (zero,) * modes)
            for k in range(modes):
                entry[mode_rows(k, h), :] = states[k]
        end_mine[...] = entry[...].astype(jnp.bfloat16)

    def state_copies(sign, send, recv, slot):
        return [
            remote(
                end_mine,
                end_in.at[slot, d - 1],
                send.at[d - 1],
                recv.at[d - 1],
                {"ctx": ctx_at(sign * d)},
            )
            for d in range(1, n)
        ]

    def enter(slot, position):
        total = jnp.zeros(entry.shape, jnp.float32)
        for d in range(1, n):
            term = end_in[slot, d - 1].astype(jnp.float32)
            if d > 1:
                term = term * jnp.exp(-rates_ref[...] * float(L * (d - 1)))
            total = total + jnp.where(position >= d, term, 0.0)
        entry[...] = total

    def run(reverse):
        for h in range(halves):
            lam = [jnp.exp(-rates_ref[mode_rows(k, h), :]) for k in range(modes)]
            gain = [scaled_ref[mode_rows(k, h), :] for k in range(modes)]

            def step(t, states):
                for u in range(2):
                    at = 2 * t + u
                    if reverse:
                        at = L - 1 - at
                    here = pl.ds(pl.multiple_of(at * ncb + h * 8, 8), 8)
                    x = seq_in[here, :]
                    states = tuple(a * s + x for a, s in zip(lam, states))
                    terms = [g * s for g, s in zip(gain, states)]
                    sums = [terms[m] for m in range(4)]
                    for m in range(4, modes):
                        sums[m % 4] = sums[m % 4] + terms[m]
                    seq_out[here, :] = (sums[0] + sums[1]) + (sums[2] + sums[3])
                return states

            first = tuple(entry[mode_rows(k, h), :] for k in range(modes))
            lax.fori_loop(0, L // 2, step, first)

    last_state(False)
    forward_states = state_copies(1, state_send, state_recv, 0)
    for copy in forward_states:
        copy.start()

    for copy in cot_copies:
        copy.wait_recv()

    tile = min(256, C)

    def grad_tile(i, carry):
        col = cols_of(i, tile)
        value = lax.dot_general(
            cot_all[...],
            w_ref[col, :],
            (((1,), (1,)), ((), ())),
            preferred_element_type=jnp.float32,
        )
        part[:, col] = value.astype(jnp.bfloat16)
        return carry

    lax.fori_loop(0, C // tile, grad_tile, 0)
    rs_copies = [
        remote(
            part.at[rows_of(ctx_at(d)), :],
            part_in.at[d - 1],
            rs_send.at[d - 1],
            rs_recv.at[d - 1],
            {"ctx": ctx_at(d)},
        )
        for d in range(1, n)
    ]
    for copy in rs_copies:
        copy.start()

    for copy in forward_states:
        copy.wait_recv()
    enter(0, c)
    run(False)

    def product_block(i, carry):
        mixed = seq_out[pl.ds(i, L, stride=ncb), :]
        prod_all[rows_of(c), cols_of(i)] = (conv[i] * mixed).astype(jnp.bfloat16)
        return carry

    lax.fori_loop(0, ncb, product_block, 0)
    ag_copies = [
        remote(
            prod_all.at[rows_of(c), :],
            prod_all.at[rows_of(c), :],
            ag_send.at[d - 1],
            ag_recv.at[d - 1],
            {"ctx": ctx_at(d)},
        )
        for d in range(1, n)
    ]
    for copy in ag_copies:
        copy.start()

    for copy in forward_states:
        copy.wait_send()
    for copy in rs_copies:
        copy.wait_recv()

    def grad_block(i, carry):
        col = cols_of(i)
        grad = part[rows_of(c), col].astype(jnp.float32)
        for d in range(1, n):
            grad = grad + part_in[d - 1, :, col].astype(jnp.float32)
        mixed = seq_out[pl.ds(i, L, stride=ncb), :]
        ge[i, 0:L, :] = grad * mixed
        ghalo_mine[0, :, col] = (grad * mixed)[0:16].astype(jnp.bfloat16)
        seq_in[pl.ds(i, L, stride=ncb), :] = grad * conv[i]
        return carry

    lax.fori_loop(0, ncb, grad_block, 0)
    last_state(True)
    backward_states = state_copies(-1, adj_send, adj_recv, 1)
    for copy in backward_states:
        copy.start()

    for copy in ag_copies:
        copy.wait_recv()
    otile = min(256, N)

    def out_tile(i, carry):
        col = cols_of(i, otile)
        value = jnp.dot(prod_all[...], w_ref[:, col], preferred_element_type=jnp.float32)
        opart[:, col] = value.astype(jnp.bfloat16)
        return carry

    lax.fori_loop(0, N // otile, out_tile, 0)
    ors_copies = [
        remote(
            opart.at[rows_of(tp_at(d)), :],
            opart_in.at[d - 1],
            ors_send.at[d - 1],
            ors_recv.at[d - 1],
            {"tp": tp_at(d)},
        )
        for d in range(1, n)
    ]
    for copy in ors_copies:
        copy.start()

    for copy in backward_states:
        copy.wait_recv()
    enter(1, n - 1 - c)
    run(True)

    def gated_block(i, carry):
        col = cols_of(i)
        grad = seq_out[pl.ds(i, L, stride=ncb), :]
        for b, other in ((1, 2), (2, 1)):
            value = grad * conv[other * ncb + i]
            ge[b * ncb + i, 0:L, :] = value
            ghalo_mine[b, :, col] = value[0:16].astype(jnp.bfloat16)
        return carry

    lax.fori_loop(0, ncb, gated_block, 0)
    gh_copy = remote(ghalo_mine, ghalo, gh_send, gh_recv, {"ctx": ctx_at(-1)})

    @pl.when(c > 0)
    def _():
        gh_copy.start()

    for copy in ors_copies:
        copy.wait_recv()
    total = opart[rows_of(p), :].astype(jnp.float32)
    for d in range(1, n):
        total = total + opart_in[d - 1].astype(jnp.float32)
    osum[...] = total.astype(jnp.bfloat16)
    fin_turn = remote(osum, ofin, fin_sem.at[0], fin_sem.at[1], {"ctx": p, "tp": c})

    @pl.when(c != p)
    def _():
        fin_turn.start()

    fsum[...] = jnp.zeros(fsum.shape, fsum.dtype)
    group = C // fsum.shape[1]

    def filter_block(i, carry):
        lane = lax.broadcasted_iota(jnp.int32, (LANES, fsum.shape[1]), 0) + i * LANES
        low = lax.broadcasted_iota(jnp.int32, (LANES, fsum.shape[1]), 1) * group
        member = jnp.where((lane >= low) & (lane < low + group), 1.0, 0.0)
        for b in range(3):
            at = b * ncb + i
            grad = ge[at, 0:L, :]
            for j in range(taps):
                fs_mine[b * 8 + j : b * 8 + j + 1, :] = jnp.sum(
                    grad * xp[at, 8 - j : 8 - j + L, :], axis=0, keepdims=True
                )
        fsum[...] += jnp.dot(
            fs_mine[...],
            member,
            precision=lax.Precision.HIGHEST,
            preferred_element_type=jnp.float32,
        )
        return carry

    fs_mine[...] = jnp.zeros(fs_mine.shape, fs_mine.dtype)
    lax.fori_loop(0, ncb, filter_block, 0)
    fs_copies = [
        remote(
            fsum, fs_in.at[d - 1], fs_send.at[d - 1], fs_recv.at[d - 1], {"ctx": ctx_at(d)}
        )
        for d in range(1, n)
    ]
    for copy in fs_copies:
        copy.start()

    @pl.when(c == n - 1)
    def _():
        ghalo[...] = jnp.zeros(ghalo.shape, ghalo.dtype)

    @pl.when(c < n - 1)
    def _():
        gh_copy.wait_recv()

    def input_block(i, carry):
        col = cols_of(i)
        for b, g_ref in enumerate((gq_ref, gk_ref, gv_ref)):
            at = b * ncb + i
            ge[at, L : L + 8, :] = ghalo[b, :, col].astype(jnp.float32)[0:8]
            acc = taps_ref[b, 0:1, col] * ge[at, 0:L, :]
            for j in range(1, taps):
                acc = acc + taps_ref[b, j : j + 1, col] * ge[at, j : j + L, :]
            g_ref[:, col] = acc.astype(jnp.bfloat16)
        return carry

    lax.fori_loop(0, ncb, input_block, 0)

    for copy in fs_copies:
        copy.wait_recv()
    sums = fsum[...]
    for d in range(1, n):
        sums = sums + fs_in[d - 1]
    gs_ref[...] = sums / float(L * n)

    @pl.when(c != p)
    def _():
        fin_turn.wait_recv()
        out_ref[...] = ofin[...]

    @pl.when(c == p)
    def _():
        out_ref[...] = osum[...]

    @pl.when(c != p)
    def _():
        cot_turn.wait_send()
        fin_turn.wait_send()

    @pl.when(c < n - 1)
    def _():
        for copy in halo_copies:
            copy.wait_send()

    @pl.when(c > 0)
    def _():
        gh_copy.wait_send()

    for copy in cot_copies + rs_copies + ag_copies + backward_states + ors_copies + fs_copies:
        copy.wait_send()


def fused_shards(n, q_in, k_in, v_in, short_filters, rates, residues, out_weight, cotangent):
    L, C = q_in.shape
    N = out_weight.shape[1]
    modes = rates.shape[0]
    groups, taps = short_filters.shape[1:]
    ncb = C // LANES
    rows = modes * ncb
    filter_rows = jnp.repeat(jnp.transpose(short_filters, (0, 2, 1)), C // groups, axis=2)
    scaled = residues * jnp.sqrt(-jnp.expm1(-2.0 * rates))
    bf16, f32 = jnp.bfloat16, jnp.float32
    dma = pltpu.SemaphoreType.DMA
    vmem = pl.BlockSpec(memory_space=pltpu.VMEM)
    m = n - 1
    outs = pl.pallas_call(
        functools.partial(fused_kernel, n),
        out_shape=(
            jax.ShapeDtypeStruct((L, N), bf16),
            jax.ShapeDtypeStruct((L, C), bf16),
            jax.ShapeDtypeStruct((L, C), bf16),
            jax.ShapeDtypeStruct((L, C), bf16),
            jax.ShapeDtypeStruct((24, groups), f32),
        ),
        in_specs=[vmem] * 8,
        out_specs=(vmem,) * 5,
        scratch_shapes=[
            pltpu.VMEM((3, 16, C), bf16),
            pltpu.VMEM((3 * ncb, L + 8, LANES), f32),
            pltpu.VMEM((3 * ncb, L, LANES), f32),
            pltpu.VMEM((L * ncb, LANES), f32),
            pltpu.VMEM((L * ncb, LANES), f32),
            pltpu.VMEM((rows, LANES), bf16),
            pltpu.VMEM((2, m, rows, LANES), bf16),
            pltpu.VMEM((rows, LANES), f32),
            pltpu.VMEM((n * L, N), bf16),
            pltpu.VMEM((n * L, C), bf16),
            pltpu.VMEM((m, L, C), bf16),
            pltpu.VMEM((n * L, C), bf16),
            pltpu.VMEM((n * L, N), bf16),
            pltpu.VMEM((m, L, N), bf16),
            pltpu.VMEM((L, N), bf16),
            pltpu.VMEM((L, N), bf16),
            pltpu.VMEM((3 * ncb, L + 8, LANES), f32),
            pltpu.VMEM((3, 16, C), bf16),
            pltpu.VMEM((3, 16, C), bf16),
            pltpu.VMEM((24, groups), f32),
            pltpu.VMEM((24, LANES), f32),
            pltpu.VMEM((m, 24, groups), f32),
            dma((3,)),
            dma((m,)),
            dma((m,)),
            dma((3,)),
            dma((3,)),
            dma((m,)),
            dma((m,)),
            dma((m,)),
            dma((m,)),
            dma((m,)),
            dma((m,)),
            dma((m,)),
            dma((m,)),
            dma((m,)),
            dma((m,)),
            dma((2,)),
            dma,
            dma,
            dma((m,)),
            dma((m,)),
        ],
        compiler_params=pltpu.CompilerParams(
            collective_id=0, has_side_effects=True, vmem_limit_bytes=56 * 1024 * 1024
        ),
    )(
        q_in,
        k_in,
        v_in,
        filter_rows,
        rates.reshape(rows, LANES),
        scaled.reshape(rows, LANES),
        out_weight,
        cotangent,
    )
    grad_short = jnp.transpose(outs[4].reshape(3, 8, groups)[:, :taps], (0, 2, 1))
    return outs[:4] + (grad_short,)


def solution(mesh):
    placed = (
        P(("groups", "ctx"), "tp"),
        P(("groups", "ctx"), "tp"),
        P(("groups", "ctx"), "tp"),
        P(None, "tp", None),
        P(None, "tp"),
        P(None, "tp"),
        P("tp", "ctx"),
        P(("groups", "ctx"), "tp"),
    )
    n = mesh.shape["ctx"]
    body = shards
    if n == mesh.shape["tp"] == 4:
        body = functools.partial(fused_shards, n)
    return jax.shard_map(
        body,
        mesh=mesh,
        in_specs=placed,
        out_specs=(
            P(("groups", "ctx"), "tp"),
            P(("groups", "ctx"), "tp"),
            P(("groups", "ctx"), "tp"),
            P(("groups", "ctx"), "tp"),
            P("groups", "tp", None),
        ),
        check_vma=False,
    )
```

```python
import functools

import jax
import jax.numpy as jnp
from jax import lax
from jax.experimental import pallas as pl
from jax.experimental.pallas import tpu as pltpu
from jax.sharding import PartitionSpec as P

block_rows = 16


def shifted(shard, axis, by):
    length = lax.axis_size(axis)
    pairs = [(i, i + by) for i in range(length) if 0 <= i + by < length]
    return lax.ppermute(shard, axis, pairs)


def entering(shard, axis, combine, identity, reverse):
    length, index = (lax.axis_size(axis), lax.axis_index(axis))
    everything = jax.tree.map(
        lambda part, kind: lax.all_gather(part.astype(kind), axis),
        shard,
        (jnp.bfloat16, jnp.bfloat16),
    )
    start = jax.tree.map(
        lambda part, zero: jnp.broadcast_to(jnp.asarray(zero, part.dtype), part.shape),
        shard,
        identity,
    )

    def lap(k, before):
        at = length - 1 - k if reverse else k
        reached = at > index if reverse else at < index
        new = combine(
            before, jax.tree.map(lambda part, own: part[at].astype(own.dtype), everything, shard)
        )
        return jax.tree.map(lambda a, b: jnp.where(reached, a, b), new, before)

    return lax.fori_loop(0, length, lap, start)


def shortened(shard):
    return jax.tree.map(lambda a: a.astype(jnp.bfloat16) if a.dtype == jnp.float32 else a, shard)


def chain_link(earlier, following):
    return (earlier[0] * following[0], following[0] * earlier[1] + following[1])


def shards(q_in, k_in, v_in, short_filters, rates, residues, out_weight, cotangent):
    length, channels = q_in.shape
    filter_taps = short_filters.shape[2]
    group_count = short_filters.shape[1]
    group_size = channels // group_count
    blocks = length // block_rows
    sequence = length * lax.axis_size("ctx")
    highest = lax.Precision.HIGHEST
    stacked = jnp.stack([q_in, k_in, v_in])
    front_rows = shifted(stacked[:, length - filter_taps + 1 :, :], "ctx", 1)
    extended = jnp.concatenate([front_rows, stacked], axis=1).astype(jnp.float32)
    filter_rows = jnp.repeat(short_filters, group_size, axis=1)
    convolved = jnp.zeros((3, length, channels), jnp.float32)
    for shift_by in range(filter_taps):
        start = filter_taps - 1 - shift_by
        convolved = (
            convolved + filter_rows[:, None, :, shift_by] * extended[:, start : start + length, :]
        )
    query_conv = convolved[0]
    key_conv = convolved[1]
    value_conv = convolved[2]
    gated = key_conv * value_conv
    offsets = jnp.arange(block_rows, dtype=jnp.float32)
    scaled = residues * jnp.sqrt(-jnp.expm1(-2.0 * rates))
    powers = jnp.exp(-rates[None] * offsets[:, None, None])
    kernel = jnp.sum(powers * scaled[None], axis=1)
    lag_table = (
        jnp.arange(block_rows, dtype=jnp.int32)[:, None]
        - jnp.arange(block_rows, dtype=jnp.int32)[None, :]
    )
    toeplitz = jnp.where((lag_table >= 0)[:, :, None], kernel[jnp.maximum(lag_table, 0)], 0.0)
    end_powers = jnp.exp(-rates[None] * (block_rows - 1.0 - offsets)[:, None, None])
    lead_powers = scaled[None] * jnp.exp(-rates[None] * (offsets + 1.0)[:, None, None])
    tail_powers = scaled[None] * jnp.exp(-rates[None] * (block_rows - offsets)[:, None, None])
    block_index = jnp.arange(blocks, dtype=jnp.float32)
    block_decay = jnp.broadcast_to(jnp.exp(-rates * block_rows)[None], (blocks,) + rates.shape)
    entry_decay = jnp.exp(-rates[None] * (block_rows * block_index)[:, None, None])
    exit_decay = jnp.exp(-rates[None] * (block_rows * (blocks - 1.0 - block_index))[:, None, None])
    piece_decay = jnp.exp(-rates * length)
    identity = (jnp.ones_like(rates), jnp.zeros_like(rates))
    gated_blocks = gated.reshape(blocks, block_rows, channels)
    block_states = jnp.einsum("snc,bsc->bnc", end_powers, gated_blocks, precision=highest)
    prefix = lax.associative_scan(chain_link, (block_decay, block_states), axis=0)[1]
    local_end = prefix[-1]
    state_in = entering((piece_decay, local_end), "ctx", chain_link, identity, False)[1]
    earlier_states = jnp.concatenate([jnp.zeros_like(prefix[:1]), prefix[:-1]], axis=0)
    entry_states = earlier_states + entry_decay * state_in[None]
    mixed = jnp.einsum("tsc,bsc->btc", toeplitz, gated_blocks, precision=highest)
    mixed = mixed + jnp.einsum("tnc,bnc->btc", lead_powers, entry_states, precision=highest)
    mixed = mixed.reshape(length, channels)
    product = (query_conv * mixed).astype(jnp.bfloat16)
    weights = lax.all_gather(out_weight, "ctx", axis=1, tiled=True)
    partial_value = jnp.dot(product, weights, preferred_element_type=jnp.float32)
    output = lax.psum_scatter(
        partial_value.astype(jnp.bfloat16), "tp", scatter_dimension=1, tiled=True
    )
    seed = lax.all_gather(cotangent, "tp", axis=1, tiled=True)
    grad_product = lax.dot_general(
        seed, weights, (((1,), (1,)), ((), ())), preferred_element_type=jnp.float32
    )
    grad_query = grad_product * mixed
    grad_mixed = (grad_product * query_conv).reshape(blocks, block_rows, channels)
    block_adjoint = jnp.einsum("snc,bsc->bnc", powers, grad_mixed, precision=highest)
    suffix = lax.associative_scan(chain_link, (block_decay, block_adjoint), reverse=True, axis=0)[1]
    local_begin = suffix[0]
    adjoint_in = entering((piece_decay, local_begin), "ctx", chain_link, identity, True)[1]
    later_adjoint = jnp.concatenate([suffix[1:], jnp.zeros_like(suffix[:1])], axis=0)
    exit_adjoint = later_adjoint + exit_decay * adjoint_in[None]
    grad_gated = jnp.einsum("tsc,btc->bsc", toeplitz, grad_mixed, precision=highest)
    grad_gated = grad_gated + jnp.einsum(
        "snc,bnc->bsc", tail_powers, exit_adjoint, precision=highest
    )
    grad_gated = grad_gated.reshape(length, channels)
    grads = jnp.stack([grad_query, grad_gated * value_conv, grad_gated * key_conv])
    back_rows = shifted(shortened(grads[:, : filter_taps - 1, :]), "ctx", -1)
    grad_extended = jnp.concatenate([grads, back_rows], axis=1)
    input_grads = jnp.zeros((3, length, channels), jnp.float32)
    filter_terms = []
    for shift_by in range(filter_taps):
        input_grads = (
            input_grads
            + filter_rows[:, None, :, shift_by] * grad_extended[:, shift_by : shift_by + length, :]
        )
        start = filter_taps - 1 - shift_by
        filter_terms.append(jnp.sum(grads * extended[:, start : start + length, :], axis=1))
    local_filter = jnp.stack(filter_terms, axis=1)
    local_filter = (
        jnp.sum(local_filter.reshape(3, filter_taps, group_count, group_size), axis=3) / sequence
    )
    local_filter = jnp.transpose(local_filter, (0, 2, 1))
    grad_short = lax.psum(local_filter, "ctx")
    input_grads = input_grads.astype(jnp.bfloat16)
    return (output, input_grads[0], input_grads[1], input_grads[2], grad_short)


LANES = 128
MESH = pl.DeviceIdType.MESH


def remote(src, dst, send, recv, where):
    return pltpu.make_async_remote_copy(
        src_ref=src, dst_ref=dst, send_sem=send, recv_sem=recv, device_id=where, device_id_type=MESH
    )


def fused_kernel(
    n,
    q_ref,
    k_ref,
    v_ref,
    taps_ref,
    rates_ref,
    scaled_ref,
    w_ref,
    cot_ref,
    out_ref,
    gq_ref,
    gk_ref,
    gv_ref,
    gs_ref,
    halo,
    xp,
    conv,
    seq_in,
    seq_out,
    end_mine,
    end_in,
    entry,
    cot_all,
    part,
    part_in,
    prod_all,
    opart,
    opart_in,
    osum,
    ofin,
    ge,
    ghalo_mine,
    ghalo,
    fsum,
    fs_mine,
    fs_in,
    cot_sem,
    cot_send,
    cot_recv,
    halo_send,
    halo_recv,
    state_send,
    state_recv,
    adj_send,
    adj_recv,
    rs_send,
    rs_recv,
    ag_send,
    ag_recv,
    ors_send,
    ors_recv,
    fin_sem,
    gh_send,
    gh_recv,
    fs_send,
    fs_recv,
):
    c = lax.axis_index("ctx")
    p = lax.axis_index("tp")
    L, C = q_ref.shape
    N = w_ref.shape[1]
    taps = taps_ref.shape[1]
    ncb = C // LANES
    modes = rates_ref.shape[0] // ncb
    halves = ncb // 8
    m = n - 1
    inputs = (q_ref, k_ref, v_ref)

    def ctx_at(d):
        return lax.rem(c + d + n, n)

    def tp_at(d):
        return lax.rem(p + d + n, n)

    def rows_of(i):
        return pl.ds(pl.multiple_of(i * L, L), L)

    def cols_of(i, width=LANES):
        return pl.ds(pl.multiple_of(i * width, width), width)

    barrier = pltpu.get_barrier_semaphore()
    for d in range(1, n):
        pl.semaphore_signal(barrier, inc=1, device_id={"ctx": ctx_at(d)}, device_id_type=MESH)
        pl.semaphore_signal(barrier, inc=1, device_id={"tp": tp_at(d)}, device_id_type=MESH)

    @pl.when(c != p)
    def _():
        pl.semaphore_signal(barrier, inc=1, device_id={"ctx": p, "tp": c}, device_id_type=MESH)

    @pl.when(c != p)
    def _():
        pl.semaphore_wait(barrier, 2 * (n - 1) + 1)

    @pl.when(c == p)
    def _():
        pl.semaphore_wait(barrier, 2 * (n - 1))

    halo_copies = [
        remote(
            x.at[pl.ds(L - 16, 16), :],
            halo.at[b],
            halo_send.at[b],
            halo_recv.at[b],
            {"ctx": ctx_at(1)},
        )
        for b, x in enumerate(inputs)
    ]

    @pl.when(c < n - 1)
    def _():
        for copy in halo_copies:
            copy.start()

    cot_turn = remote(
        cot_ref, cot_all.at[rows_of(c), :], cot_sem.at[0], cot_sem.at[1], {"ctx": p, "tp": c}
    )
    cot_keep = pltpu.make_async_copy(cot_ref, cot_all.at[rows_of(c), :], cot_sem.at[2])

    @pl.when(c != p)
    def _():
        cot_turn.start()

    @pl.when(c == p)
    def _():
        cot_keep.start()

    @pl.when(c == 0)
    def _():
        halo[...] = jnp.zeros(halo.shape, halo.dtype)

    @pl.when(c > 0)
    def _():
        for copy in halo_copies:
            copy.wait_recv()

    def conv_block(i, carry):
        col = cols_of(i)
        done = []
        for b, x in enumerate(inputs):
            at = b * ncb + i
            xp[at, 0:8, :] = halo[b, :, col].astype(jnp.float32)[8:16]
            xp[at, 8 : 8 + L, :] = x[:, col].astype(jnp.float32)
            acc = taps_ref[b, 0:1, col] * xp[at, 8 : 8 + L, :]
            for j in range(1, taps):
                acc = acc + taps_ref[b, j : j + 1, col] * xp[at, 8 - j : 8 - j + L, :]
            conv[at] = acc
            done.append(acc)
        seq_in[pl.ds(i, L, stride=ncb), :] = done[1] * done[2]
        return carry

    half_blocks = ncb // 2
    lax.fori_loop(0, half_blocks, conv_block, 0)

    @pl.when(c != p)
    def _():
        cot_turn.wait_recv()

    @pl.when(c == p)
    def _():
        cot_keep.wait()

    cot_copies = [
        remote(
            cot_all.at[rows_of(p), :],
            cot_all.at[rows_of(p), :],
            cot_send.at[d - 1],
            cot_recv.at[d - 1],
            {"tp": tp_at(d)},
        )
        for d in range(1, n)
    ]
    for copy in cot_copies:
        copy.start()

    lax.fori_loop(half_blocks, ncb, conv_block, 0)

    def mode_rows(k, h):
        return pl.ds(k * ncb + h * 8, 8)

    def last_state(reverse):
        for h in range(halves):
            lam = [jnp.exp(-rates_ref[mode_rows(k, h), :]) for k in range(modes)]

            def step(t, states):
                for u in range(4):
                    at = 4 * t + u
                    if reverse:
                        at = L - 1 - at
                    x = seq_in[pl.ds(pl.multiple_of(at * ncb + h * 8, 8), 8), :]
                    states = tuple(a * s + x for a, s in zip(lam, states))
                return states

            zero = jnp.zeros((8, LANES), jnp.float32)
            states = lax.fori_loop(0, L // 4, step, (zero,) * modes)
            for k in range(modes):
                entry[mode_rows(k, h), :] = states[k]
        end_mine[...] = entry[...].astype(jnp.bfloat16)

    def state_copies(sign, send, recv, slot):
        return [
            remote(
                end_mine,
                end_in.at[slot, d - 1],
                send.at[d - 1],
                recv.at[d - 1],
                {"ctx": ctx_at(sign * d)},
            )
            for d in range(1, n)
        ]

    def enter(slot, position):
        total = jnp.zeros(entry.shape, jnp.float32)
        for d in range(1, n):
            term = end_in[slot, d - 1].astype(jnp.float32)
            if d > 1:
                term = term * jnp.exp(-rates_ref[...] * float(L * (d - 1)))
            total = total + jnp.where(position >= d, term, 0.0)
        entry[...] = total

    def run(reverse):
        for h in range(halves):
            lam = [jnp.exp(-rates_ref[mode_rows(k, h), :]) for k in range(modes)]
            gain = [scaled_ref[mode_rows(k, h), :] for k in range(modes)]

            def step(t, states):
                for u in range(2):
                    at = 2 * t + u
                    if reverse:
                        at = L - 1 - at
                    here = pl.ds(pl.multiple_of(at * ncb + h * 8, 8), 8)
                    x = seq_in[here, :]
                    states = tuple(a * s + x for a, s in zip(lam, states))
                    terms = [g * s for g, s in zip(gain, states)]
                    sums = terms[:4]
                    for k in range(4, modes):
                        sums[k % 4] = sums[k % 4] + terms[k]
                    seq_out[here, :] = (sums[0] + sums[1]) + (sums[2] + sums[3])
                return states

            first = tuple(entry[mode_rows(k, h), :] for k in range(modes))
            lax.fori_loop(0, L // 2, step, first)

    last_state(False)
    forward_states = state_copies(1, state_send, state_recv, 0)
    for copy in forward_states:
        copy.start()

    for copy in cot_copies:
        copy.wait_recv()

    tile = min(256, C)

    def grad_tile(i, carry):
        col = cols_of(i, tile)
        value = lax.dot_general(
            cot_all[...],
            w_ref[col, :],
            (((1,), (1,)), ((), ())),
            preferred_element_type=jnp.float32,
        )
        part[:, col] = value.astype(jnp.bfloat16)
        return carry

    lax.fori_loop(0, C // tile, grad_tile, 0)

    def place(way):
        return c if way == 0 else n - 1 - c

    def rs_chunk(way, at):
        return at if way == 0 else n - 1 - at

    def rs_copy(way, s):
        return remote(
            part.at[rows_of(rs_chunk(way, n - 1 - s + place(way))), :],
            part_in.at[way * m + s],
            rs_send.at[way * m + s],
            rs_recv.at[way * m + s],
            {"ctx": ctx_at(1 - 2 * way)},
        )

    def rs_sends(way, s):
        return (place(way) < n - 1) & (place(way) <= s)

    def rs_start(s):
        for way in range(2):

            @pl.when(rs_sends(way, s))
            def _():
                rs_copy(way, s).start()

    def rs_arrive(s):
        for way in range(2):

            @pl.when((place(way) > 0) & (place(way) <= s + 1))
            def _():
                pltpu.make_async_remote_copy(
                    src_ref=part_in.at[way * m + s],
                    dst_ref=part_in.at[way * m + s],
                    send_sem=rs_send.at[way * m + s],
                    recv_sem=rs_recv.at[way * m + s],
                    device_id={"ctx": ctx_at(1 - 2 * way)},
                    device_id_type=MESH,
                ).wait_recv()
                if s < m - 1:
                    mine = rows_of(rs_chunk(way, n - 2 - s + place(way)))

                    def add_block(i, carry):
                        col = cols_of(i)
                        value = part[mine, col].astype(jnp.float32)
                        value = value + part_in[way * m + s, :, col].astype(jnp.float32)
                        part[mine, col] = value.astype(jnp.bfloat16)
                        return carry

                    lax.fori_loop(0, ncb, add_block, 0)

    def ag_copy(way, s, back):
        rows = rows_of(c - (1 - 2 * way) * (s + back))
        return remote(
            prod_all.at[rows, :],
            prod_all.at[rows, :],
            ag_send.at[way * m + s],
            ag_recv.at[way * m + s],
            {"ctx": ctx_at(1 - 2 * way)},
        )

    def ag_sends(way, s):
        return (place(way) < n - 1) & (place(way) >= s)

    def ag_start(s):
        for way in range(2):

            @pl.when(ag_sends(way, s))
            def _():
                ag_copy(way, s, 0).start()

    def ag_arrive(s):
        for way in range(2):

            @pl.when(place(way) > s)
            def _():
                ag_copy(way, s, 1).wait_recv()

    @pl.when(c == 0)
    def _():
        part_in[m - 1] = jnp.zeros((L, C), jnp.bfloat16)

    @pl.when(c == n - 1)
    def _():
        part_in[2 * m - 1] = jnp.zeros((L, C), jnp.bfloat16)

    rs_start(0)

    for copy in forward_states:
        copy.wait_recv()
    enter(0, c)
    run(False)

    def product_block(i, carry):
        mixed = seq_out[pl.ds(i, L, stride=ncb), :]
        prod_all[rows_of(c), cols_of(i)] = (conv[i] * mixed).astype(jnp.bfloat16)
        return carry

    lax.fori_loop(0, ncb, product_block, 0)
    ag_start(0)
    for copy in forward_states:
        copy.wait_send()
    for hop in range(1, m):
        rs_arrive(hop - 1)
        rs_start(hop)
        ag_arrive(hop - 1)
        ag_start(hop)
    rs_arrive(m - 1)

    def grad_block(i, carry):
        col = cols_of(i)
        grad = part[rows_of(c), col].astype(jnp.float32)
        for way in range(2):
            grad = grad + part_in[way * m + m - 1, :, col].astype(jnp.float32)
        mixed = seq_out[pl.ds(i, L, stride=ncb), :]
        ge[i, 0:L, :] = grad * mixed
        ghalo_mine[0, :, col] = (grad * mixed)[0:16].astype(jnp.bfloat16)
        seq_in[pl.ds(i, L, stride=ncb), :] = grad * conv[i]
        return carry

    lax.fori_loop(0, ncb, grad_block, 0)
    last_state(True)
    backward_states = state_copies(-1, adj_send, adj_recv, 1)
    for copy in backward_states:
        copy.start()

    ag_arrive(m - 1)
    otile = min(256, N)

    def out_tile(i, carry):
        col = cols_of(i, otile)
        value = jnp.dot(prod_all[...], w_ref[:, col], preferred_element_type=jnp.float32)
        opart[:, col] = value.astype(jnp.bfloat16)
        return carry

    lax.fori_loop(0, N // otile, out_tile, 0)
    ors_copies = [
        remote(
            opart.at[rows_of(tp_at(d)), :],
            opart_in.at[d - 1],
            ors_send.at[d - 1],
            ors_recv.at[d - 1],
            {"tp": tp_at(d)},
        )
        for d in range(1, n)
    ]
    for copy in ors_copies:
        copy.start()

    for copy in backward_states:
        copy.wait_recv()
    enter(1, n - 1 - c)
    run(True)

    def gated_block(i, carry):
        col = cols_of(i)
        grad = seq_out[pl.ds(i, L, stride=ncb), :]
        for b, other in ((1, 2), (2, 1)):
            value = grad * conv[other * ncb + i]
            ge[b * ncb + i, 0:L, :] = value
            ghalo_mine[b, :, col] = value[0:16].astype(jnp.bfloat16)
        return carry

    lax.fori_loop(0, ncb, gated_block, 0)
    gh_copy = remote(ghalo_mine, ghalo, gh_send, gh_recv, {"ctx": ctx_at(-1)})

    @pl.when(c > 0)
    def _():
        gh_copy.start()

    for copy in ors_copies:
        copy.wait_recv()
    total = opart[rows_of(p), :].astype(jnp.float32)
    for d in range(1, n):
        total = total + opart_in[d - 1].astype(jnp.float32)
    osum[...] = total.astype(jnp.bfloat16)
    fin_turn = remote(osum, ofin, fin_sem.at[0], fin_sem.at[1], {"ctx": p, "tp": c})

    @pl.when(c != p)
    def _():
        fin_turn.start()

    fsum[...] = jnp.zeros(fsum.shape, fsum.dtype)
    group = C // fsum.shape[1]

    def filter_block(i, carry):
        lane = lax.broadcasted_iota(jnp.int32, (LANES, fsum.shape[1]), 0) + i * LANES
        low = lax.broadcasted_iota(jnp.int32, (LANES, fsum.shape[1]), 1) * group
        member = jnp.where((lane >= low) & (lane < low + group), 1.0, 0.0)
        for b in range(3):
            at = b * ncb + i
            grad = ge[at, 0:L, :]
            for j in range(taps):
                fs_mine[b * 8 + j : b * 8 + j + 1, :] = jnp.sum(
                    grad * xp[at, 8 - j : 8 - j + L, :], axis=0, keepdims=True
                )
        fsum[...] += jnp.dot(
            fs_mine[...],
            member,
            precision=lax.Precision.HIGHEST,
            preferred_element_type=jnp.float32,
        )
        return carry

    fs_mine[...] = jnp.zeros(fs_mine.shape, fs_mine.dtype)
    lax.fori_loop(0, ncb, filter_block, 0)
    fs_copies = [
        remote(
            fsum, fs_in.at[d - 1], fs_send.at[d - 1], fs_recv.at[d - 1], {"ctx": ctx_at(d)}
        )
        for d in range(1, n)
    ]
    for copy in fs_copies:
        copy.start()

    @pl.when(c == n - 1)
    def _():
        ghalo[...] = jnp.zeros(ghalo.shape, ghalo.dtype)

    @pl.when(c < n - 1)
    def _():
        gh_copy.wait_recv()

    def input_block(i, carry):
        col = cols_of(i)
        for b, g_ref in enumerate((gq_ref, gk_ref, gv_ref)):
            at = b * ncb + i
            ge[at, L : L + 8, :] = ghalo[b, :, col].astype(jnp.float32)[0:8]
            acc = taps_ref[b, 0:1, col] * ge[at, 0:L, :]
            for j in range(1, taps):
                acc = acc + taps_ref[b, j : j + 1, col] * ge[at, j : j + L, :]
            g_ref[:, col] = acc.astype(jnp.bfloat16)
        return carry

    lax.fori_loop(0, ncb, input_block, 0)

    for copy in fs_copies:
        copy.wait_recv()
    sums = fsum[...]
    for d in range(1, n):
        sums = sums + fs_in[d - 1]
    gs_ref[...] = sums / float(L * n)

    @pl.when(c != p)
    def _():
        fin_turn.wait_recv()
        out_ref[...] = ofin[...]

    @pl.when(c == p)
    def _():
        out_ref[...] = osum[...]

    @pl.when(c != p)
    def _():
        cot_turn.wait_send()
        fin_turn.wait_send()

    @pl.when(c < n - 1)
    def _():
        for copy in halo_copies:
            copy.wait_send()

    @pl.when(c > 0)
    def _():
        gh_copy.wait_send()

    for hop in range(m):
        for way in range(2):

            @pl.when(rs_sends(way, hop))
            def _():
                rs_copy(way, hop).wait_send()

            @pl.when(ag_sends(way, hop))
            def _():
                ag_copy(way, hop, 0).wait_send()

    for copy in cot_copies + backward_states + ors_copies + fs_copies:
        copy.wait_send()


def fused_shards(n, q_in, k_in, v_in, short_filters, rates, residues, out_weight, cotangent):
    L, C = q_in.shape
    N = out_weight.shape[1]
    modes = rates.shape[0]
    groups, taps = short_filters.shape[1:]
    ncb = C // LANES
    rows = modes * ncb
    filter_rows = jnp.repeat(jnp.transpose(short_filters, (0, 2, 1)), C // groups, axis=2)
    scaled = residues * jnp.sqrt(-jnp.expm1(-2.0 * rates))
    bf16, f32 = jnp.bfloat16, jnp.float32
    dma = pltpu.SemaphoreType.DMA
    vmem = pl.BlockSpec(memory_space=pltpu.VMEM)
    m = n - 1
    outs = pl.pallas_call(
        functools.partial(fused_kernel, n),
        out_shape=(
            jax.ShapeDtypeStruct((L, N), bf16),
            jax.ShapeDtypeStruct((L, C), bf16),
            jax.ShapeDtypeStruct((L, C), bf16),
            jax.ShapeDtypeStruct((L, C), bf16),
            jax.ShapeDtypeStruct((24, groups), f32),
        ),
        in_specs=[vmem] * 8,
        out_specs=(vmem,) * 5,
        scratch_shapes=[
            pltpu.VMEM((3, 16, C), bf16),
            pltpu.VMEM((3 * ncb, L + 8, LANES), f32),
            pltpu.VMEM((3 * ncb, L, LANES), f32),
            pltpu.VMEM((L * ncb, LANES), f32),
            pltpu.VMEM((L * ncb, LANES), f32),
            pltpu.VMEM((rows, LANES), bf16),
            pltpu.VMEM((2, m, rows, LANES), bf16),
            pltpu.VMEM((rows, LANES), f32),
            pltpu.VMEM((n * L, N), bf16),
            pltpu.VMEM((n * L, C), bf16),
            pltpu.VMEM((2 * m, L, C), bf16),
            pltpu.VMEM((n * L, C), bf16),
            pltpu.VMEM((n * L, N), bf16),
            pltpu.VMEM((m, L, N), bf16),
            pltpu.VMEM((L, N), bf16),
            pltpu.VMEM((L, N), bf16),
            pltpu.VMEM((3 * ncb, L + 8, LANES), f32),
            pltpu.VMEM((3, 16, C), bf16),
            pltpu.VMEM((3, 16, C), bf16),
            pltpu.VMEM((24, groups), f32),
            pltpu.VMEM((24, LANES), f32),
            pltpu.VMEM((m, 24, groups), f32),
            dma((3,)),
            dma((m,)),
            dma((m,)),
            dma((3,)),
            dma((3,)),
            dma((m,)),
            dma((m,)),
            dma((m,)),
            dma((m,)),
            dma((2 * m,)),
            dma((2 * m,)),
            dma((2 * m,)),
            dma((2 * m,)),
            dma((m,)),
            dma((m,)),
            dma((2,)),
            dma,
            dma,
            dma((m,)),
            dma((m,)),
        ],
        compiler_params=pltpu.CompilerParams(
            collective_id=0, has_side_effects=True, vmem_limit_bytes=56 * 1024 * 1024
        ),
    )(
        q_in,
        k_in,
        v_in,
        filter_rows,
        rates.reshape(rows, LANES),
        scaled.reshape(rows, LANES),
        out_weight,
        cotangent,
    )
    grad_short = jnp.transpose(outs[4].reshape(3, 8, groups)[:, :taps], (0, 2, 1))
    return outs[:4] + (grad_short,)


def solution(mesh):
    placed = (
        P(("groups", "ctx"), "tp"),
        P(("groups", "ctx"), "tp"),
        P(("groups", "ctx"), "tp"),
        P(None, "tp", None),
        P(None, "tp"),
        P(None, "tp"),
        P("tp", "ctx"),
        P(("groups", "ctx"), "tp"),
    )
    n = mesh.shape["ctx"]
    body = shards
    if n == mesh.shape["tp"] == 4:
        body = functools.partial(fused_shards, n)
    return jax.shard_map(
        body,
        mesh=mesh,
        in_specs=placed,
        out_specs=(
            P(("groups", "ctx"), "tp"),
            P(("groups", "ctx"), "tp"),
            P(("groups", "ctx"), "tp"),
            P(("groups", "ctx"), "tp"),
            P("groups", "tp", None),
        ),
        check_vma=False,
    )
```

```python
import functools

import jax
import jax.numpy as jnp
from jax import lax
from jax.experimental import pallas as pl
from jax.experimental.pallas import tpu as pltpu
from jax.sharding import PartitionSpec as P

block_rows = 16


def shifted(shard, axis, by):
    length = lax.axis_size(axis)
    pairs = [(i, i + by) for i in range(length) if 0 <= i + by < length]
    return lax.ppermute(shard, axis, pairs)


def entering(shard, axis, combine, identity, reverse):
    length, index = (lax.axis_size(axis), lax.axis_index(axis))
    everything = jax.tree.map(
        lambda part, kind: lax.all_gather(part.astype(kind), axis),
        shard,
        (jnp.bfloat16, jnp.bfloat16),
    )
    start = jax.tree.map(
        lambda part, zero: jnp.broadcast_to(jnp.asarray(zero, part.dtype), part.shape),
        shard,
        identity,
    )

    def lap(k, before):
        at = length - 1 - k if reverse else k
        reached = at > index if reverse else at < index
        new = combine(
            before, jax.tree.map(lambda part, own: part[at].astype(own.dtype), everything, shard)
        )
        return jax.tree.map(lambda a, b: jnp.where(reached, a, b), new, before)

    return lax.fori_loop(0, length, lap, start)


def shortened(shard):
    return jax.tree.map(lambda a: a.astype(jnp.bfloat16) if a.dtype == jnp.float32 else a, shard)


def chain_link(earlier, following):
    return (earlier[0] * following[0], following[0] * earlier[1] + following[1])


def shards(q_in, k_in, v_in, short_filters, rates, residues, out_weight, cotangent):
    length, channels = q_in.shape
    filter_taps = short_filters.shape[2]
    group_count = short_filters.shape[1]
    group_size = channels // group_count
    blocks = length // block_rows
    sequence = length * lax.axis_size("ctx")
    highest = lax.Precision.HIGHEST
    stacked = jnp.stack([q_in, k_in, v_in])
    front_rows = shifted(stacked[:, length - filter_taps + 1 :, :], "ctx", 1)
    extended = jnp.concatenate([front_rows, stacked], axis=1).astype(jnp.float32)
    filter_rows = jnp.repeat(short_filters, group_size, axis=1)
    convolved = jnp.zeros((3, length, channels), jnp.float32)
    for shift_by in range(filter_taps):
        start = filter_taps - 1 - shift_by
        convolved = (
            convolved + filter_rows[:, None, :, shift_by] * extended[:, start : start + length, :]
        )
    query_conv = convolved[0]
    key_conv = convolved[1]
    value_conv = convolved[2]
    gated = key_conv * value_conv
    offsets = jnp.arange(block_rows, dtype=jnp.float32)
    scaled = residues * jnp.sqrt(-jnp.expm1(-2.0 * rates))
    powers = jnp.exp(-rates[None] * offsets[:, None, None])
    kernel = jnp.sum(powers * scaled[None], axis=1)
    lag_table = (
        jnp.arange(block_rows, dtype=jnp.int32)[:, None]
        - jnp.arange(block_rows, dtype=jnp.int32)[None, :]
    )
    toeplitz = jnp.where((lag_table >= 0)[:, :, None], kernel[jnp.maximum(lag_table, 0)], 0.0)
    end_powers = jnp.exp(-rates[None] * (block_rows - 1.0 - offsets)[:, None, None])
    lead_powers = scaled[None] * jnp.exp(-rates[None] * (offsets + 1.0)[:, None, None])
    tail_powers = scaled[None] * jnp.exp(-rates[None] * (block_rows - offsets)[:, None, None])
    block_index = jnp.arange(blocks, dtype=jnp.float32)
    block_decay = jnp.broadcast_to(jnp.exp(-rates * block_rows)[None], (blocks,) + rates.shape)
    entry_decay = jnp.exp(-rates[None] * (block_rows * block_index)[:, None, None])
    exit_decay = jnp.exp(-rates[None] * (block_rows * (blocks - 1.0 - block_index))[:, None, None])
    piece_decay = jnp.exp(-rates * length)
    identity = (jnp.ones_like(rates), jnp.zeros_like(rates))
    gated_blocks = gated.reshape(blocks, block_rows, channels)
    block_states = jnp.einsum("snc,bsc->bnc", end_powers, gated_blocks, precision=highest)
    prefix = lax.associative_scan(chain_link, (block_decay, block_states), axis=0)[1]
    local_end = prefix[-1]
    state_in = entering((piece_decay, local_end), "ctx", chain_link, identity, False)[1]
    earlier_states = jnp.concatenate([jnp.zeros_like(prefix[:1]), prefix[:-1]], axis=0)
    entry_states = earlier_states + entry_decay * state_in[None]
    mixed = jnp.einsum("tsc,bsc->btc", toeplitz, gated_blocks, precision=highest)
    mixed = mixed + jnp.einsum("tnc,bnc->btc", lead_powers, entry_states, precision=highest)
    mixed = mixed.reshape(length, channels)
    product = (query_conv * mixed).astype(jnp.bfloat16)
    weights = lax.all_gather(out_weight, "ctx", axis=1, tiled=True)
    partial_value = jnp.dot(product, weights, preferred_element_type=jnp.float32)
    output = lax.psum_scatter(
        partial_value.astype(jnp.bfloat16), "tp", scatter_dimension=1, tiled=True
    )
    seed = lax.all_gather(cotangent, "tp", axis=1, tiled=True)
    grad_product = lax.dot_general(
        seed, weights, (((1,), (1,)), ((), ())), preferred_element_type=jnp.float32
    )
    grad_query = grad_product * mixed
    grad_mixed = (grad_product * query_conv).reshape(blocks, block_rows, channels)
    block_adjoint = jnp.einsum("snc,bsc->bnc", powers, grad_mixed, precision=highest)
    suffix = lax.associative_scan(chain_link, (block_decay, block_adjoint), reverse=True, axis=0)[1]
    local_begin = suffix[0]
    adjoint_in = entering((piece_decay, local_begin), "ctx", chain_link, identity, True)[1]
    later_adjoint = jnp.concatenate([suffix[1:], jnp.zeros_like(suffix[:1])], axis=0)
    exit_adjoint = later_adjoint + exit_decay * adjoint_in[None]
    grad_gated = jnp.einsum("tsc,btc->bsc", toeplitz, grad_mixed, precision=highest)
    grad_gated = grad_gated + jnp.einsum(
        "snc,bnc->bsc", tail_powers, exit_adjoint, precision=highest
    )
    grad_gated = grad_gated.reshape(length, channels)
    grads = jnp.stack([grad_query, grad_gated * value_conv, grad_gated * key_conv])
    back_rows = shifted(shortened(grads[:, : filter_taps - 1, :]), "ctx", -1)
    grad_extended = jnp.concatenate([grads, back_rows], axis=1)
    input_grads = jnp.zeros((3, length, channels), jnp.float32)
    filter_terms = []
    for shift_by in range(filter_taps):
        input_grads = (
            input_grads
            + filter_rows[:, None, :, shift_by] * grad_extended[:, shift_by : shift_by + length, :]
        )
        start = filter_taps - 1 - shift_by
        filter_terms.append(jnp.sum(grads * extended[:, start : start + length, :], axis=1))
    local_filter = jnp.stack(filter_terms, axis=1)
    local_filter = (
        jnp.sum(local_filter.reshape(3, filter_taps, group_count, group_size), axis=3) / sequence
    )
    local_filter = jnp.transpose(local_filter, (0, 2, 1))
    grad_short = lax.psum(local_filter, "ctx")
    input_grads = input_grads.astype(jnp.bfloat16)
    return (output, input_grads[0], input_grads[1], input_grads[2], grad_short)


LANES = 128
MESH = pl.DeviceIdType.MESH


def remote(src, dst, send, recv, where):
    return pltpu.make_async_remote_copy(
        src_ref=src, dst_ref=dst, send_sem=send, recv_sem=recv, device_id=where, device_id_type=MESH
    )


def fused_kernel(
    n,
    q_ref,
    k_ref,
    v_ref,
    taps_ref,
    rates_ref,
    scaled_ref,
    w_ref,
    cot_ref,
    out_ref,
    gq_ref,
    gk_ref,
    gv_ref,
    gs_ref,
    halo,
    xp,
    conv,
    seq_in,
    seq_out,
    end_mine,
    end_in,
    entry,
    cot_all,
    part,
    part_in,
    prod_all,
    opart,
    opart_in,
    osum,
    ofin,
    ge,
    ghalo_mine,
    ghalo,
    fsum,
    fs_mine,
    fs_in,
    cot_sem,
    cot_send,
    cot_recv,
    halo_send,
    halo_recv,
    state_send,
    state_recv,
    adj_send,
    adj_recv,
    rs_send,
    rs_recv,
    ag_send,
    ag_recv,
    ors_send,
    ors_recv,
    fin_sem,
    gh_send,
    gh_recv,
    fs_send,
    fs_recv,
):
    c = lax.axis_index("ctx")
    p = lax.axis_index("tp")
    L, C = q_ref.shape
    N = w_ref.shape[1]
    taps = taps_ref.shape[1]
    ncb = C // LANES
    modes = rates_ref.shape[0] // ncb
    halves = ncb // 8
    m = n - 1
    inputs = (q_ref, k_ref, v_ref)

    def ctx_at(d):
        return lax.rem(c + d + n, n)

    def tp_at(d):
        return lax.rem(p + d + n, n)

    def rows_of(i):
        return pl.ds(pl.multiple_of(i * L, L), L)

    def cols_of(i, width=LANES):
        return pl.ds(pl.multiple_of(i * width, width), width)

    barrier = pltpu.get_barrier_semaphore()
    for d in range(1, n):
        pl.semaphore_signal(barrier, inc=1, device_id={"ctx": ctx_at(d)}, device_id_type=MESH)
        pl.semaphore_signal(barrier, inc=1, device_id={"tp": tp_at(d)}, device_id_type=MESH)

    @pl.when(c != p)
    def _():
        pl.semaphore_signal(barrier, inc=1, device_id={"ctx": p, "tp": c}, device_id_type=MESH)

    @pl.when(c != p)
    def _():
        pl.semaphore_wait(barrier, 2 * (n - 1) + 1)

    @pl.when(c == p)
    def _():
        pl.semaphore_wait(barrier, 2 * (n - 1))

    halo_copies = [
        remote(
            x.at[pl.ds(L - 16, 16), :],
            halo.at[b],
            halo_send.at[b],
            halo_recv.at[b],
            {"ctx": ctx_at(1)},
        )
        for b, x in enumerate(inputs)
    ]

    @pl.when(c < n - 1)
    def _():
        for copy in halo_copies:
            copy.start()

    cot_turn = remote(
        cot_ref, cot_all.at[rows_of(c), :], cot_sem.at[0], cot_sem.at[1], {"ctx": p, "tp": c}
    )
    cot_keep = pltpu.make_async_copy(cot_ref, cot_all.at[rows_of(c), :], cot_sem.at[2])

    @pl.when(c != p)
    def _():
        cot_turn.start()

    @pl.when(c == p)
    def _():
        cot_keep.start()

    @pl.when(c == 0)
    def _():
        halo[...] = jnp.zeros(halo.shape, halo.dtype)

    @pl.when(c > 0)
    def _():
        for copy in halo_copies:
            copy.wait_recv()

    def conv_block(i, carry):
        col = cols_of(i)
        done = []
        for b, x in enumerate(inputs):
            at = b * ncb + i
            xp[at, 0:8, :] = halo[b, :, col].astype(jnp.float32)[8:16]
            xp[at, 8 : 8 + L, :] = x[:, col].astype(jnp.float32)
            acc = taps_ref[b, 0:1, col] * xp[at, 8 : 8 + L, :]
            for j in range(1, taps):
                acc = acc + taps_ref[b, j : j + 1, col] * xp[at, 8 - j : 8 - j + L, :]
            conv[at] = acc
            done.append(acc)
        seq_in[pl.ds(i, L, stride=ncb), :] = done[1] * done[2]
        return carry

    half_blocks = ncb // 2
    lax.fori_loop(0, half_blocks, conv_block, 0)

    @pl.when(c != p)
    def _():
        cot_turn.wait_recv()

    @pl.when(c == p)
    def _():
        cot_keep.wait()

    other = p + 1 - 2 * lax.rem(p, 2)
    cot_copies = [
        remote(
            cot_all.at[rows_of(block), :],
            cot_all.at[rows_of(block), :],
            cot_send.at[at],
            cot_recv.at[at],
            {"tp": to},
        )
        for at, (block, to) in enumerate(((p, tp_at(2)), (p, other), (tp_at(2), other)))
    ]
    cot_copies[0].start()
    cot_copies[1].start()

    lax.fori_loop(half_blocks, ncb, conv_block, 0)

    def mode_rows(k, h):
        return pl.ds(k * ncb + h * 8, 8)

    def last_state(reverse):
        for h in range(halves):
            lam = [jnp.exp(-rates_ref[mode_rows(k, h), :]) for k in range(modes)]

            def step(t, states):
                for u in range(4):
                    at = 4 * t + u
                    if reverse:
                        at = L - 1 - at
                    x = seq_in[pl.ds(pl.multiple_of(at * ncb + h * 8, 8), 8), :]
                    states = tuple(a * s + x for a, s in zip(lam, states))
                return states

            zero = jnp.zeros((8, LANES), jnp.float32)
            states = lax.fori_loop(0, L // 4, step, (zero,) * modes)
            for k in range(modes):
                entry[mode_rows(k, h), :] = states[k]
        end_mine[...] = entry[...].astype(jnp.bfloat16)

    def state_copies(sign, send, recv, slot):
        return [
            remote(
                end_mine,
                end_in.at[slot, d - 1],
                send.at[d - 1],
                recv.at[d - 1],
                {"ctx": ctx_at(sign * d)},
            )
            for d in range(1, n)
        ]

    def enter(slot, position):
        total = jnp.zeros(entry.shape, jnp.float32)
        for d in range(1, n):
            term = end_in[slot, d - 1].astype(jnp.float32)
            if d > 1:
                term = term * jnp.exp(-rates_ref[...] * float(L * (d - 1)))
            total = total + jnp.where(position >= d, term, 0.0)
        entry[...] = total

    def run(reverse):
        for h in range(halves):
            lam = [jnp.exp(-rates_ref[mode_rows(k, h), :]) for k in range(modes)]
            gain = [scaled_ref[mode_rows(k, h), :] for k in range(modes)]

            def step(t, states):
                for u in range(2):
                    at = 2 * t + u
                    if reverse:
                        at = L - 1 - at
                    here = pl.ds(pl.multiple_of(at * ncb + h * 8, 8), 8)
                    x = seq_in[here, :]
                    states = tuple(a * s + x for a, s in zip(lam, states))
                    terms = [g * s for g, s in zip(gain, states)]
                    sums = terms[:4]
                    for k in range(4, modes):
                        sums[k % 4] = sums[k % 4] + terms[k]
                    seq_out[here, :] = (sums[0] + sums[1]) + (sums[2] + sums[3])
                return states

            first = tuple(entry[mode_rows(k, h), :] for k in range(modes))
            lax.fori_loop(0, L // 2, step, first)

    cot_copies[0].wait_recv()
    cot_copies[2].start()
    last_state(False)
    forward_states = state_copies(1, state_send, state_recv, 0)
    for copy in forward_states:
        copy.start()

    for copy in cot_copies[1:]:
        copy.wait_recv()

    tile = min(256, C)

    def grad_tile(i, carry):
        col = cols_of(i, tile)
        value = lax.dot_general(
            cot_all[...],
            w_ref[col, :],
            (((1,), (1,)), ((), ())),
            preferred_element_type=jnp.float32,
        )
        part[:, col] = value.astype(jnp.bfloat16)
        return carry

    lax.fori_loop(0, C // tile, grad_tile, 0)

    def place(way):
        return c if way == 0 else n - 1 - c

    def rs_chunk(way, at):
        return at if way == 0 else n - 1 - at

    def rs_copy(way, s):
        return remote(
            part.at[rows_of(rs_chunk(way, n - 1 - s + place(way))), :],
            part_in.at[way * m + s],
            rs_send.at[way * m + s],
            rs_recv.at[way * m + s],
            {"ctx": ctx_at(1 - 2 * way)},
        )

    def rs_sends(way, s):
        return (place(way) < n - 1) & (place(way) <= s)

    def rs_start(s):
        for way in range(2):

            @pl.when(rs_sends(way, s))
            def _():
                rs_copy(way, s).start()

    def rs_arrive(s):
        for way in range(2):

            @pl.when((place(way) > 0) & (place(way) <= s + 1))
            def _():
                pltpu.make_async_remote_copy(
                    src_ref=part_in.at[way * m + s],
                    dst_ref=part_in.at[way * m + s],
                    send_sem=rs_send.at[way * m + s],
                    recv_sem=rs_recv.at[way * m + s],
                    device_id={"ctx": ctx_at(1 - 2 * way)},
                    device_id_type=MESH,
                ).wait_recv()
                if s < m - 1:
                    mine = rows_of(rs_chunk(way, n - 2 - s + place(way)))

                    def add_block(i, carry):
                        col = cols_of(i)
                        value = part[mine, col].astype(jnp.float32)
                        value = value + part_in[way * m + s, :, col].astype(jnp.float32)
                        part[mine, col] = value.astype(jnp.bfloat16)
                        return carry

                    lax.fori_loop(0, ncb, add_block, 0)

    def ag_copy(way, s, back):
        rows = rows_of(c - (1 - 2 * way) * (s + back))
        return remote(
            prod_all.at[rows, :],
            prod_all.at[rows, :],
            ag_send.at[way * m + s],
            ag_recv.at[way * m + s],
            {"ctx": ctx_at(1 - 2 * way)},
        )

    def ag_sends(way, s):
        return (place(way) < n - 1) & (place(way) >= s)

    def ag_start(s):
        for way in range(2):

            @pl.when(ag_sends(way, s))
            def _():
                ag_copy(way, s, 0).start()

    def ag_arrive(s):
        for way in range(2):

            @pl.when(place(way) > s)
            def _():
                ag_copy(way, s, 1).wait_recv()

    @pl.when(c == 0)
    def _():
        part_in[m - 1] = jnp.zeros((L, C), jnp.bfloat16)

    @pl.when(c == n - 1)
    def _():
        part_in[2 * m - 1] = jnp.zeros((L, C), jnp.bfloat16)

    rs_start(0)

    for copy in forward_states:
        copy.wait_recv()
    enter(0, c)
    run(False)

    def product_block(i, carry):
        mixed = seq_out[pl.ds(i, L, stride=ncb), :]
        prod_all[rows_of(c), cols_of(i)] = (conv[i] * mixed).astype(jnp.bfloat16)
        return carry

    lax.fori_loop(0, ncb, product_block, 0)
    ag_start(0)
    for copy in forward_states:
        copy.wait_send()
    for hop in range(1, m):
        rs_arrive(hop - 1)
        rs_start(hop)
        ag_arrive(hop - 1)
        ag_start(hop)
    rs_arrive(m - 1)

    def grad_block(i, carry):
        col = cols_of(i)
        grad = part[rows_of(c), col].astype(jnp.float32)
        for way in range(2):
            grad = grad + part_in[way * m + m - 1, :, col].astype(jnp.float32)
        mixed = seq_out[pl.ds(i, L, stride=ncb), :]
        ge[i, 0:L, :] = grad * mixed
        ghalo_mine[0, :, col] = (grad * mixed)[0:16].astype(jnp.bfloat16)
        seq_in[pl.ds(i, L, stride=ncb), :] = grad * conv[i]
        return carry

    lax.fori_loop(0, ncb, grad_block, 0)
    last_state(True)
    backward_states = state_copies(-1, adj_send, adj_recv, 1)
    for copy in backward_states:
        copy.start()

    ag_arrive(m - 1)
    otile = min(256, N)

    def out_tile(i, carry):
        col = cols_of(i, otile)
        value = jnp.dot(prod_all[...], w_ref[:, col], preferred_element_type=jnp.float32)
        opart[:, col] = value.astype(jnp.bfloat16)
        return carry

    lax.fori_loop(0, N // otile, out_tile, 0)
    ors_copies = [
        remote(
            opart.at[rows_of(tp_at(d)), :],
            opart_in.at[d - 1],
            ors_send.at[d - 1],
            ors_recv.at[d - 1],
            {"tp": tp_at(d)},
        )
        for d in range(1, n)
    ]
    for copy in ors_copies:
        copy.start()

    for copy in backward_states:
        copy.wait_recv()
    enter(1, n - 1 - c)
    run(True)

    def gated_block(i, carry):
        col = cols_of(i)
        grad = seq_out[pl.ds(i, L, stride=ncb), :]
        for b, other in ((1, 2), (2, 1)):
            value = grad * conv[other * ncb + i]
            ge[b * ncb + i, 0:L, :] = value
            ghalo_mine[b, :, col] = value[0:16].astype(jnp.bfloat16)
        return carry

    lax.fori_loop(0, ncb, gated_block, 0)
    gh_copy = remote(ghalo_mine, ghalo, gh_send, gh_recv, {"ctx": ctx_at(-1)})

    @pl.when(c > 0)
    def _():
        gh_copy.start()

    for copy in ors_copies:
        copy.wait_recv()
    total = opart[rows_of(p), :].astype(jnp.float32)
    for d in range(1, n):
        total = total + opart_in[d - 1].astype(jnp.float32)
    osum[...] = total.astype(jnp.bfloat16)
    fin_turn = remote(osum, ofin, fin_sem.at[0], fin_sem.at[1], {"ctx": p, "tp": c})

    @pl.when(c != p)
    def _():
        fin_turn.start()

    fsum[...] = jnp.zeros(fsum.shape, fsum.dtype)
    group = C // fsum.shape[1]

    def filter_block(i, carry):
        lane = lax.broadcasted_iota(jnp.int32, (LANES, fsum.shape[1]), 0) + i * LANES
        low = lax.broadcasted_iota(jnp.int32, (LANES, fsum.shape[1]), 1) * group
        member = jnp.where((lane >= low) & (lane < low + group), 1.0, 0.0)
        for b in range(3):
            at = b * ncb + i
            grad = ge[at, 0:L, :]
            for j in range(taps):
                fs_mine[b * 8 + j : b * 8 + j + 1, :] = jnp.sum(
                    grad * xp[at, 8 - j : 8 - j + L, :], axis=0, keepdims=True
                )
        fsum[...] += jnp.dot(
            fs_mine[...],
            member,
            precision=lax.Precision.HIGHEST,
            preferred_element_type=jnp.float32,
        )
        return carry

    fs_mine[...] = jnp.zeros(fs_mine.shape, fs_mine.dtype)
    lax.fori_loop(0, ncb, filter_block, 0)
    fs_copies = [
        remote(
            fsum, fs_in.at[d - 1], fs_send.at[d - 1], fs_recv.at[d - 1], {"ctx": ctx_at(d)}
        )
        for d in range(1, n)
    ]
    for copy in fs_copies:
        copy.start()

    @pl.when(c == n - 1)
    def _():
        ghalo[...] = jnp.zeros(ghalo.shape, ghalo.dtype)

    @pl.when(c < n - 1)
    def _():
        gh_copy.wait_recv()

    def input_block(i, carry):
        col = cols_of(i)
        for b, g_ref in enumerate((gq_ref, gk_ref, gv_ref)):
            at = b * ncb + i
            ge[at, L : L + 8, :] = ghalo[b, :, col].astype(jnp.float32)[0:8]
            acc = taps_ref[b, 0:1, col] * ge[at, 0:L, :]
            for j in range(1, taps):
                acc = acc + taps_ref[b, j : j + 1, col] * ge[at, j : j + L, :]
            g_ref[:, col] = acc.astype(jnp.bfloat16)
        return carry

    lax.fori_loop(0, ncb, input_block, 0)

    for copy in fs_copies:
        copy.wait_recv()
    sums = fsum[...]
    for d in range(1, n):
        sums = sums + fs_in[d - 1]
    gs_ref[...] = sums / float(L * n)

    @pl.when(c != p)
    def _():
        fin_turn.wait_recv()
        out_ref[...] = ofin[...]

    @pl.when(c == p)
    def _():
        out_ref[...] = osum[...]

    @pl.when(c != p)
    def _():
        cot_turn.wait_send()
        fin_turn.wait_send()

    @pl.when(c < n - 1)
    def _():
        for copy in halo_copies:
            copy.wait_send()

    @pl.when(c > 0)
    def _():
        gh_copy.wait_send()

    for hop in range(m):
        for way in range(2):

            @pl.when(rs_sends(way, hop))
            def _():
                rs_copy(way, hop).wait_send()

            @pl.when(ag_sends(way, hop))
            def _():
                ag_copy(way, hop, 0).wait_send()

    for copy in cot_copies + backward_states + ors_copies + fs_copies:
        copy.wait_send()


def fused_shards(n, q_in, k_in, v_in, short_filters, rates, residues, out_weight, cotangent):
    L, C = q_in.shape
    N = out_weight.shape[1]
    modes = rates.shape[0]
    groups, taps = short_filters.shape[1:]
    ncb = C // LANES
    rows = modes * ncb
    filter_rows = jnp.repeat(jnp.transpose(short_filters, (0, 2, 1)), C // groups, axis=2)
    scaled = residues * jnp.sqrt(-jnp.expm1(-2.0 * rates))
    bf16, f32 = jnp.bfloat16, jnp.float32
    dma = pltpu.SemaphoreType.DMA
    vmem = pl.BlockSpec(memory_space=pltpu.VMEM)
    m = n - 1
    outs = pl.pallas_call(
        functools.partial(fused_kernel, n),
        out_shape=(
            jax.ShapeDtypeStruct((L, N), bf16),
            jax.ShapeDtypeStruct((L, C), bf16),
            jax.ShapeDtypeStruct((L, C), bf16),
            jax.ShapeDtypeStruct((L, C), bf16),
            jax.ShapeDtypeStruct((24, groups), f32),
        ),
        in_specs=[vmem] * 8,
        out_specs=(vmem,) * 5,
        scratch_shapes=[
            pltpu.VMEM((3, 16, C), bf16),
            pltpu.VMEM((3 * ncb, L + 8, LANES), f32),
            pltpu.VMEM((3 * ncb, L, LANES), f32),
            pltpu.VMEM((L * ncb, LANES), f32),
            pltpu.VMEM((L * ncb, LANES), f32),
            pltpu.VMEM((rows, LANES), bf16),
            pltpu.VMEM((2, m, rows, LANES), bf16),
            pltpu.VMEM((rows, LANES), f32),
            pltpu.VMEM((n * L, N), bf16),
            pltpu.VMEM((n * L, C), bf16),
            pltpu.VMEM((2 * m, L, C), bf16),
            pltpu.VMEM((n * L, C), bf16),
            pltpu.VMEM((n * L, N), bf16),
            pltpu.VMEM((m, L, N), bf16),
            pltpu.VMEM((L, N), bf16),
            pltpu.VMEM((L, N), bf16),
            pltpu.VMEM((3 * ncb, L + 8, LANES), f32),
            pltpu.VMEM((3, 16, C), bf16),
            pltpu.VMEM((3, 16, C), bf16),
            pltpu.VMEM((24, groups), f32),
            pltpu.VMEM((24, LANES), f32),
            pltpu.VMEM((m, 24, groups), f32),
            dma((3,)),
            dma((m,)),
            dma((m,)),
            dma((3,)),
            dma((3,)),
            dma((m,)),
            dma((m,)),
            dma((m,)),
            dma((m,)),
            dma((2 * m,)),
            dma((2 * m,)),
            dma((2 * m,)),
            dma((2 * m,)),
            dma((m,)),
            dma((m,)),
            dma((2,)),
            dma,
            dma,
            dma((m,)),
            dma((m,)),
        ],
        compiler_params=pltpu.CompilerParams(
            collective_id=0, has_side_effects=True, vmem_limit_bytes=56 * 1024 * 1024
        ),
    )(
        q_in,
        k_in,
        v_in,
        filter_rows,
        rates.reshape(rows, LANES),
        scaled.reshape(rows, LANES),
        out_weight,
        cotangent,
    )
    grad_short = jnp.transpose(outs[4].reshape(3, 8, groups)[:, :taps], (0, 2, 1))
    return outs[:4] + (grad_short,)


def solution(mesh):
    placed = (
        P(("groups", "ctx"), "tp"),
        P(("groups", "ctx"), "tp"),
        P(("groups", "ctx"), "tp"),
        P(None, "tp", None),
        P(None, "tp"),
        P(None, "tp"),
        P("tp", "ctx"),
        P(("groups", "ctx"), "tp"),
    )
    n = mesh.shape["ctx"]
    body = shards
    if n == mesh.shape["tp"] == 4:
        body = functools.partial(fused_shards, n)
    return jax.shard_map(
        body,
        mesh=mesh,
        in_specs=placed,
        out_specs=(
            P(("groups", "ctx"), "tp"),
            P(("groups", "ctx"), "tp"),
            P(("groups", "ctx"), "tp"),
            P(("groups", "ctx"), "tp"),
            P("groups", "tp", None),
        ),
        check_vma=False,
    )
```
